256 devices in a mesh: blk: 128 (over x_hi, z, y, core), rep: 2 (over x_lo).
Axes of the slice: x: 4 (x_hi: 2, x_lo: 2; x = x_hi * 2 + x_lo), y: 4, z: 8, core: 2. Of those that a mesh axis runs over, the one named last changes fastest.
Arguments:
- activations: bfloat16 [256, 8192], P(('blk', 'rep')), may hold values from -6 to 6
- out_cotangent: bfloat16 [256, 8192], P(('blk', 'rep')), may hold values from -6 to 6
- gate_blocks: bfloat16 [256, 72, 4096], P('blk'), may hold values from -0.09375 to 0.09375
- up_blocks: bfloat16 [256, 72, 4096], P('blk'), may hold values from -0.09375 to 0.09375
- down_blocks: bfloat16 [256, 72, 4096], P('blk'), may hold values from -0.0625 to 0.0625
- block_index: int32 [3, 256, 72], P(None, 'blk'), may hold values from 0 to 127, as said below
- block_counts: int32 [3, 256], P(None, 'blk'), may hold values from 56 to 72, as said below
Outputs:
- layer_out: bfloat16 [256, 8192], P(('blk', 'rep'))
- input_grad: bfloat16 [256, 8192], P(('blk', 'rep'))
- gate_grad: float32 [256, 72, 4096], P('blk', 'rep')
- up_grad: float32 [256, 72, 4096], P('blk', 'rep')
- down_grad: float32 [256, 72, 4096], P('blk', 'rep')
The draws below stay inside these ranges and needn't reach their ends.
Inputs may be any that keep to these rules, and one draw needn't show every extreme that they name: `block_index`: for each list the first block_counts entries are distinct model-width block numbers and the remaining entries are 0. `block_counts`: each of the three matrices has a list with exactly 72 live entries, at a hidden block drawn from the seed.
All inputs are finite; a program needn't handle non-finite values.
Results may differ from the reference program's by a relative error of at most 0.01.
Values may be sent and summed in bfloat16 or wider, within the bound.
No kernel may reach another device: no remote copies, remote signals or barrier semaphores. Data moves between devices by JAX's collectives and lax.ppermute only.
A program may use at most 128 MiB of HBM per device.

```python
import jax
import jax.numpy as jnp
from jax import lax

D = 8192
FF = 16384
BS = 64
TOKENS = 256
NDB = 128
FBLK = 256
MAXB = 72
MINB = 56


def pattern_common(key):
    key_counts, key_top, key_perm = jax.random.split(key, 3)
    counts = jax.random.randint(key_counts, (3, FBLK), MINB, MAXB + 1)
    top_column = jax.random.randint(key_top, (3,), 0, FBLK)
    counts = jnp.where(jnp.arange(FBLK)[None, :] == top_column[:, None], MAXB, counts)
    perm_keys = jax.random.split(key_perm, 3 * FBLK)
    orders = jax.vmap(lambda single: jax.random.permutation(single, NDB))(perm_keys)
    orders = orders.reshape(3, FBLK, NDB)[:, :, :MAXB]
    index = jnp.where(jnp.arange(MAXB)[None, None, :] < counts[:, :, None], orders, 0)
    return (index.astype(jnp.int32), counts.astype(jnp.int32))


def draw_block_index(key, part):
    index, counts = pattern_common(key)
    return index


def draw_block_counts(key, part):
    index, counts = pattern_common(key)
    return counts


def level_of(rng, extent, cuts, least, high):
    factor_of, own = 1.0, jax.random.fold_in(rng, 6)
    for dim, shards_of in cuts:
        draws = jnp.exp(jax.random.uniform(jax.random.fold_in(own, dim), (shards_of,), jnp.float32, least / len(cuts), high / len(cuts)))
        factor_of = factor_of * jnp.repeat(draws, extent[dim] // shards_of).reshape([-1 if axis == dim else 1 for axis in range(len(extent))])
    return factor_of


def noise(stream_key, dims, width, limit, shards=(), kind=jnp.bfloat16):
    values = width * jax.random.normal(stream_key, dims, jnp.float32)
    if shards:
        values = values * level_of(stream_key, dims, shards, -0.22, 0.18)
    return jnp.clip(values, -limit, limit).astype(kind)


def setup_inputs(seed: int = 0) -> dict:
    keys = jax.random.split(jax.random.key(seed), 8)
    return {
        "activations": noise(keys[0], (TOKENS, D), 1.0, 6.0, ((0, 256),)),
        "out_cotangent": noise(keys[1], (TOKENS, D), 1.0, 6.0, ((0, 256),)),
        "gate_blocks": noise(keys[2], (FBLK, MAXB, BS * BS), (D // 2) ** -0.5, 0.09375, ((0, 128),)),
        "up_blocks": noise(keys[3], (FBLK, MAXB, BS * BS), (D // 2) ** -0.5, 0.09375, ((0, 128),)),
        "down_blocks": noise(keys[4], (FBLK, MAXB, BS * BS), (FF // 2) ** -0.5, 0.0625, ((0, 128),)),
        "block_index": draw_block_index(jax.random.fold_in(keys[7], 71), 0),
        "block_counts": draw_block_counts(jax.random.fold_in(keys[7], 71), 0),
    }


def round_half(values):
    return lax.optimization_barrier(values.astype(jnp.bfloat16)).astype(jnp.float32)


def reference(activations, out_cotangent, gate_blocks, up_blocks, down_blocks, block_index, block_counts):
    row_total = activations.shape[0]
    block_count = D // BS
    input_blocks = activations.reshape(row_total, block_count, BS)
    cot_blocks = out_cotangent.reshape(row_total, block_count, BS)

    def column(carried, column_item):
        out_acc, grad_acc = carried
        w_gate, w_up, w_down, lists, counts = column_item
        live_mask = (jnp.arange(MAXB)[None, :] < counts[:, None]).astype(jnp.float32)
        w_gate = w_gate.reshape(MAXB, BS, BS).astype(jnp.float32) * live_mask[0][:, None, None]
        w_up = w_up.reshape(MAXB, BS, BS).astype(jnp.float32) * live_mask[1][:, None, None]
        w_down = w_down.reshape(MAXB, BS, BS).astype(jnp.float32) * live_mask[2][:, None, None]
        gate_inputs = input_blocks[:, lists[0]].astype(jnp.float32)
        up_inputs = input_blocks[:, lists[1]].astype(jnp.float32)
        gate = jnp.einsum("tbi,bij->tj", gate_inputs, w_gate)
        upper = jnp.einsum("tbi,bij->tj", up_inputs, w_up)
        sigmoid_gate = jax.nn.sigmoid(gate)
        activation = gate * sigmoid_gate
        hidden = round_half(activation * upper)
        out_acc = out_acc.at[:, lists[2]].add(jnp.einsum("tj,bjk->tbk", hidden, w_down))
        cot_rows = cot_blocks[:, lists[2]].astype(jnp.float32)
        hidden_grad = jnp.einsum("tbk,bjk->tj", cot_rows, w_down)
        down_part = jnp.einsum("tj,tbk->bjk", hidden, cot_rows) * live_mask[2][:, None, None]
        gate_cot = round_half(hidden_grad * upper * sigmoid_gate * (1.0 + gate * (1.0 - sigmoid_gate)))
        up_cot = round_half(hidden_grad * activation)
        gate_part = jnp.einsum("tbi,tj->bij", gate_inputs, gate_cot) * live_mask[0][:, None, None]
        up_part = jnp.einsum("tbi,tj->bij", up_inputs, up_cot) * live_mask[1][:, None, None]
        grad_acc = grad_acc.at[:, lists[0]].add(jnp.einsum("tj,bij->tbi", gate_cot, w_gate))
        grad_acc = grad_acc.at[:, lists[1]].add(jnp.einsum("tj,bij->tbi", up_cot, w_up))
        return (out_acc, grad_acc), (gate_part.reshape(MAXB, BS * BS), up_part.reshape(MAXB, BS * BS), down_part.reshape(MAXB, BS * BS))

    zeros_acc = jnp.zeros((row_total, block_count, BS), jnp.float32)
    items = (gate_blocks, up_blocks, down_blocks, jnp.transpose(block_index, (1, 0, 2)), jnp.transpose(block_counts))
    (out_acc, grad_acc), (gate_grad, up_grad, down_grad) = lax.scan(column, (zeros_acc, zeros_acc), items)
    layer_out = out_acc.reshape(row_total, D).astype(jnp.bfloat16)
    input_grad = grad_acc.reshape(row_total, D).astype(jnp.bfloat16)
    return layer_out, input_grad, gate_grad, up_grad, down_grad
```

```python
import functools

import jax
import jax.numpy as jnp
from jax import lax
from jax.experimental import pallas as pl
from jax.experimental.pallas import tpu as pltpu
from jax.sharding import Mesh
from jax.sharding import PartitionSpec as P

SIDE = 64
LANES = 128
WIDTH = SIDE * LANES
UNITS = 2 * SIDE
HALF = 36
PADDED = 40
ROWS = 16
FAR = 16
SHIFTS = (2, 1, 3)
VMEM_BYTES = 44 * 1024 * 1024
BF16 = jnp.bfloat16
F32 = jnp.float32
NT = (((1,), (1,)), ((), ()))


def call(kernel, outs, scratch, micros, *operands):
    return pl.pallas_call(
        kernel,
        out_shape=outs,
        in_specs=[pl.BlockSpec(memory_space=pltpu.VMEM)] * len(operands),
        out_specs=[pl.BlockSpec(memory_space=pltpu.VMEM)] * len(outs),
        scratch_shapes=scratch,
        compiler_params=pltpu.CompilerParams(vmem_limit_bytes=VMEM_BYTES),
        cost_estimate=pl.CostEstimate(
            flops=0, bytes_accessed=int(micros * 3_000_000), transcendentals=0
        ),
    )(*operands)


def span(step, width):
    return pl.ds(pl.multiple_of(step * width, width), width)


def densify_kernel(pick_ref, gate_ref, up_ref, down_ref, wide_ref, down_dense_ref, strip_ref):
    for matrix, blocks_ref in enumerate((gate_ref, up_ref)):

        def spread(step, carry, matrix=matrix, blocks_ref=blocks_ref):
            cols = span(step, 8 * SIDE)
            first, second = (
                jnp.dot(
                    pick_ref[2 * matrix + unit],
                    blocks_ref[unit, :, cols],
                    preferred_element_type=F32,
                )
                for unit in range(2)
            )
            for inner in range(8):
                part = slice(inner * SIDE, (inner + 1) * SIDE)
                tile = jnp.concatenate([first[:, part], second[:, part]], axis=1)
                wide_ref[
                    span(step * 8 + inner, LANES), matrix * UNITS : (matrix + 1) * UNITS
                ] = tile.astype(BF16)
            return carry

        lax.fori_loop(0, 8, spread, 0)
    for unit in range(2):

        def turn(step, carry, unit=unit):
            dense = jnp.dot(
                pick_ref[4 + unit],
                down_ref[unit, :, span(step, 256)],
                preferred_element_type=F32,
            )
            strip_ref[span(step, 256), :] = dense.T
            return carry

        lax.fori_loop(0, 16, turn, 0)
        for inner in range(SIDE):
            rows = strip_ref[pl.ds(inner, SIDE, SIDE), :]
            down_dense_ref[
                unit * SIDE : (unit + 1) * SIDE, inner * LANES : (inner + 1) * LANES
            ] = rows.astype(BF16)


def joined(pieces, which, cols):
    return jnp.concatenate([piece[which, :, cols] for piece in pieces], axis=0)


def middle_kernel(*refs):
    pieces = refs[:8]
    wide_ref, down_ref, near_ref, away_ref, hidden_ref, cots_ref, back_ref = refs[8:]

    def forward(step, total):
        cols = span(step, 1024)
        return total + jnp.dot(
            joined(pieces, 0, cols), wide_ref[cols, :], preferred_element_type=F32
        )

    both = lax.fori_loop(0, 8, forward, jnp.zeros((LANES, 2 * UNITS), F32))

    def backward(step, total):
        cols = span(step, 1024)
        return total + lax.dot_general(
            joined(pieces, 1, cols), down_ref[:, cols], NT, preferred_element_type=F32
        )

    hidden_grad = lax.fori_loop(0, 8, backward, jnp.zeros((LANES, UNITS), F32))
    gate, upper = both[:, :UNITS], both[:, UNITS:]
    sigmoid_gate = jax.nn.sigmoid(gate)
    activation = gate * sigmoid_gate
    hidden = activation * upper
    gate_cot = hidden_grad * upper * sigmoid_gate * (1.0 + gate * (1.0 - sigmoid_gate))
    up_cot = hidden_grad * activation
    hidden_ref[...] = hidden.T.astype(BF16)
    cots_ref[:UNITS, :] = gate_cot.T.astype(BF16)
    cots_ref[UNITS:, :] = up_cot.T.astype(BF16)
    hidden = hidden.astype(BF16)
    back_ref[:, :UNITS] = gate_cot.astype(BF16)
    back_ref[:, UNITS:] = up_cot.astype(BF16)

    def put(which, cols, values):
        values = values.astype(BF16)
        for slot in range(4):
            near_ref[slot, which, :, cols] = values[slot * ROWS : (slot + 1) * ROWS]
            away_ref[slot, which, :, cols] = values[(slot + 4) * ROWS : (slot + 5) * ROWS]

    def outward(step, carry):
        cols = span(step, 512)
        put(0, cols, jnp.dot(hidden, down_ref[:, cols], preferred_element_type=F32))
        put(
            1,
            cols,
            lax.dot_general(back_ref[...], wide_ref[cols, :], NT, preferred_element_type=F32),
        )
        return carry

    lax.fori_loop(0, 16, outward, 0)


def listed(select_ref, rows, cols, keep_ref, send_ref):
    values = lax.dot_general(select_ref[...], rows, NT, preferred_element_type=F32)
    keep_ref[:, cols] = values[: 2 * PADDED]
    send_ref[:, cols] = values[2 * PADDED :].astype(BF16)


def down_grad_kernel(*refs):
    pieces = refs[:8]
    hidden_ref, select_ref, keep_ref, send_ref, strip_ref = refs[8:]

    def dense(step, carry):
        values = jnp.dot(
            hidden_ref[...], joined(pieces, 1, span(step, 512)), preferred_element_type=F32
        )
        for part in range(4):
            for unit in range(2):
                strip_ref[unit, pl.ds(step * 4 + part, SIDE, SIDE), :] = values[
                    unit * SIDE : (unit + 1) * SIDE, part * LANES : (part + 1) * LANES
                ]
        return carry

    lax.fori_loop(0, 16, dense, 0)

    def pick(step, carry):
        cols = span(step, 256)
        rows = jnp.concatenate([strip_ref[0, cols, :], strip_ref[1, cols, :]], axis=1)
        listed(select_ref, rows.astype(BF16), cols, keep_ref, send_ref)
        return carry

    lax.fori_loop(0, 16, pick, 0)


def wide_grad_kernel(*refs):
    pieces = refs[:8]
    cots_ref, select_ref, keep_gate, send_gate, keep_up, send_up = refs[8:]

    def step_of(step, carry):
        values = jnp.dot(
            cots_ref[...], joined(pieces, 0, span(step, 512)), preferred_element_type=F32
        ).astype(BF16)
        for matrix, keep_ref, send_ref in ((0, keep_gate, send_gate), (1, keep_up, send_up)):
            rows = jnp.concatenate(
                [
                    jnp.concatenate(
                        [
                            values[
                                matrix * UNITS + unit * SIDE : matrix * UNITS + (unit + 1) * SIDE,
                                part * LANES : (part + 1) * LANES,
                            ]
                            for unit in range(2)
                        ],
                        axis=1,
                    )
                    for part in range(4)
                ],
                axis=0,
            )
            listed(select_ref.at[matrix], rows, span(step, 256), keep_ref, send_ref)
        return carry

    lax.fori_loop(0, 16, step_of, 0)


def ring(size, shift):
    return [(place, (place + shift) % size) for place in range(size)]


def per_device(
    activations, out_cotangent, gate_blocks, up_blocks, down_blocks, block_index, block_counts
):
    length = gate_blocks.shape[1]
    live = jnp.arange(length)[None, None, :] < block_counts[:, :, None]
    places = jnp.where(live, block_index, -1)
    pick = (places[:, :, None, :] == jnp.arange(LANES)[None, None, :, None]).astype(BF16)
    pick = pick.reshape(6, LANES, length)
    halves = jnp.pad(
        places.reshape(3, 2, 2, HALF), ((0, 0), (0, 0), (0, 0), (0, PADDED - HALF)), constant_values=-1
    )
    halves = jnp.where(lax.axis_index("rep") == 0, halves, halves[:, :, ::-1])
    halves = jnp.transpose(halves, (0, 2, 1, 3))
    goal = jnp.where(halves >= 0, halves + LANES * jnp.arange(2)[None, None, :, None], -1)
    select = (goal.reshape(3, 4 * PADDED)[:, :, None] == jnp.arange(2 * LANES)).astype(BF16)

    wide, down = call(
        densify_kernel,
        [
            jax.ShapeDtypeStruct((WIDTH, 2 * UNITS), BF16),
            jax.ShapeDtypeStruct((UNITS, WIDTH), BF16),
        ],
        [pltpu.VMEM((SIDE * SIDE, LANES), F32)],
        8,
        pick,
        gate_blocks,
        up_blocks,
        down_blocks,
    )

    rows = jnp.stack([activations, out_cotangent], axis=1).reshape(1, 2, LANES, SIDE)
    rows = jnp.swapaxes(rows, 2, 3)
    rows = lax.all_to_all(
        jnp.broadcast_to(rows, (FAR, 2, SIDE, LANES)), ("xh", "z"), 0, 0, tiled=True
    )
    first = jnp.swapaxes(rows.reshape(FAR, 2, WIDTH), 0, 1)
    here = [first] + [lax.ppermute(first, "y", ring(4, shift)) for shift in SHIFTS]
    there = [lax.ppermute(piece, "c", ring(2, 1)) for piece in here]
    pieces = here + there

    sums = jax.ShapeDtypeStruct((4, 2, ROWS, WIDTH), BF16)
    near, away, hidden, cots = call(
        middle_kernel,
        [
            sums,
            sums,
            jax.ShapeDtypeStruct((UNITS, LANES), BF16),
            jax.ShapeDtypeStruct((2 * UNITS, LANES), BF16),
        ],
        [pltpu.VMEM((LANES, 2 * UNITS), BF16)],
        8,
        *pieces,
        wide,
        down,
    )
    kept = jax.ShapeDtypeStruct((2 * PADDED, SIDE * SIDE), F32)
    sent = jax.ShapeDtypeStruct((2 * PADDED, SIDE * SIDE), BF16)

    away = lax.ppermute(away, "c", ring(2, 1))
    keep_down, send_down = call(
        down_grad_kernel,
        [kept, sent],
        [pltpu.VMEM((2, SIDE * SIDE, LANES), F32)],
        5,
        *pieces,
        hidden,
        select[2],
    )
    keep_gate, send_gate, keep_up, send_up = call(
        wide_grad_kernel, [kept, sent, kept, sent], [], 5, *pieces, cots, select[:2]
    )

    total = near.astype(F32) + away.astype(F32)
    moved = [
        lax.ppermute(total[slot + 1].astype(BF16), "y", ring(4, -shift))
        for slot, shift in enumerate(SHIFTS)
    ]
    total = total[0] + sum(part.astype(F32) for part in moved)
    total = jnp.swapaxes(total.astype(BF16), 0, 1).reshape(FAR, 2, SIDE, LANES)
    total = lax.all_to_all(total, ("xh", "z"), 0, 0, tiled=True)
    total = jnp.sum(total.astype(F32), axis=0)
    total = jnp.swapaxes(total, 1, 2).reshape(2, 1, WIDTH).astype(BF16)

    def settle(keep, send):
        other = lax.ppermute(send, "rep", ring(2, 1))
        keep, other = (
            part.reshape(2, PADDED, SIDE * SIDE)[:, :HALF] for part in (keep, other)
        )
        return keep + other.astype(F32)

    return (
        total[0],
        total[1],
        settle(keep_gate, send_gate),
        settle(keep_up, send_up),
        settle(keep_down, send_down),
    )


def solution(mesh):
    fine = Mesh(mesh.devices.reshape(2, 8, 4, 2, 2), ("xh", "z", "y", "c", "rep"))
    blk = ("xh", "z", "y", "c")
    placed = (
        P((*blk, "rep"), None),
        P((*blk, "rep"), None),
        P(blk, None, None),
        P(blk, None, None),
        P(blk, None, None),
        P(None, blk, None),
        P(None, blk),
    )
    return jax.shard_map(
        per_device,
        mesh=fine,
        in_specs=placed,
        out_specs=(
            P((*blk, "rep"), None),
            P((*blk, "rep"), None),
            P(blk, "rep", None),
            P(blk, "rep", None),
            P(blk, "rep", None),
        ),
        check_vma=False,
    )
```

```python
import functools

import jax
import jax.numpy as jnp
from jax import lax
from jax.experimental import pallas as pl
from jax.experimental.pallas import tpu as pltpu
from jax.sharding import Mesh
from jax.sharding import PartitionSpec as P

SIDE = 64
LANES = 128
WIDTH = SIDE * LANES
UNITS = 2 * SIDE
TRIPLE = 3 * UNITS
HALF = 36
KEPT = 2 * HALF
ROWS = 16
TOKENS = 4 * ROWS
FAR = 16
SHIFTS = (2, 1, 3)
VMEM_BYTES = 14 * 1024 * 1024
COST_BYTES = 30_000
BF16 = jnp.bfloat16
F32 = jnp.float32
NT = (((1,), (1,)), ((), ()))


def call(kernel, outs, scratch, micros, *operands, space=pltpu.VMEM):
    return pl.pallas_call(
        kernel,
        out_shape=outs,
        in_specs=[pl.BlockSpec(memory_space=pltpu.VMEM)] * len(operands),
        out_specs=[pl.BlockSpec(memory_space=space)] * len(outs),
        scratch_shapes=scratch,
        compiler_params=pltpu.CompilerParams(vmem_limit_bytes=VMEM_BYTES),
        cost_estimate=pl.CostEstimate(
            flops=0, bytes_accessed=int(micros * COST_BYTES), transcendentals=0
        ),
    )(*operands)


def span(step, width):
    return pl.ds(pl.multiple_of(step * width, width), width)


def densify_wide_kernel(pick_ref, gate_ref, up_ref, wide_ref):
    def spread(step, carry):
        cols = span(step, 4 * SIDE)
        for matrix, blocks_ref in enumerate((gate_ref, up_ref)):
            first, second = (
                jnp.dot(
                    pick_ref[2 * matrix + unit],
                    blocks_ref[unit, :, cols],
                    preferred_element_type=F32,
                ).astype(BF16)
                for unit in range(2)
            )
            for inner in range(4):
                part = slice(inner * SIDE, (inner + 1) * SIDE)
                wide_ref[
                    span(step * 4 + inner, LANES), matrix * UNITS : (matrix + 1) * UNITS
                ] = jnp.concatenate([first[:, part], second[:, part]], axis=1)
        return carry

    lax.fori_loop(0, 16, spread, 0, unroll=2)


def densify_down_kernel(pick_ref, down_ref, dense_ref, strip_ref):
    for unit in range(2):

        def turn(step, carry, unit=unit):
            dense = jnp.dot(
                pick_ref[4 + unit],
                down_ref[unit, :, span(step, 256)],
                preferred_element_type=F32,
            )
            strip_ref[unit, span(step, 256), :] = dense.T
            return carry

        lax.fori_loop(0, 16, turn, 0, unroll=2)

    def gather(inner, carry):
        dense_ref[:, span(inner, LANES)] = jnp.concatenate(
            [strip_ref[unit, pl.ds(inner, SIDE, SIDE), :] for unit in range(2)], axis=0
        ).astype(BF16)
        return carry

    lax.fori_loop(0, SIDE, gather, 0, unroll=8)


def joined(pieces, cols):
    return jnp.concatenate([piece[:, cols] for piece in pieces], axis=0)


def put(first_ref, moved, cols, values):
    first_ref[:, cols] = values[:ROWS]
    for slot, ref in enumerate(moved):
        ref[:, cols] = values[(slot + 1) * ROWS : (slot + 2) * ROWS].astype(BF16)


def forward_kernel(*refs):
    pieces = refs[:4]
    wides, downs = refs[4:6], refs[6:8]
    both_ref, hidden_ref, low_ref, high_ref, first_ref, *moved = refs[8:]

    def project(step, totals):
        cols = span(step, 1024)
        rows = joined(pieces, cols)
        return tuple(
            total + jnp.dot(rows, wide_ref[cols, :], preferred_element_type=F32)
            for total, wide_ref in zip(totals, wides)
        )

    zeros = jnp.zeros((TOKENS, 2 * UNITS), F32)
    totals = lax.fori_loop(0, 8, project, (zeros, zeros), unroll=2)
    hidden = []
    for core, both in enumerate(totals):
        both_ref[core] = both
        gate, upper = both[:, :UNITS], both[:, UNITS:]
        hidden.append((gate * jax.nn.sigmoid(gate) * upper).astype(BF16))
    hidden = jnp.concatenate(hidden, axis=1)
    hidden_ref[...] = hidden

    def outward(step, carry):
        cols = span(step, 512)
        weights = jnp.concatenate([down_ref[:, cols] for down_ref in downs], axis=0)
        put(first_ref, moved, cols, jnp.dot(hidden, weights, preferred_element_type=F32))
        low_ref[:, cols] = joined(pieces[:2], cols)
        high_ref[:, cols] = joined(pieces[2:], cols)
        return carry

    lax.fori_loop(0, 16, outward, 0, unroll=2)


def backward_kernel(*refs):
    pieces = refs[:4]
    wides, downs = refs[4:6], refs[6:8]
    both_ref, hidden_ref, near_ref, away_ref, first_ref, *moved, back_ref = refs[8:]

    def project(step, total):
        cols = span(step, 1024)
        weights = jnp.concatenate([down_ref[:, cols] for down_ref in downs], axis=0)
        return total + lax.dot_general(
            joined(pieces, cols), weights, NT, preferred_element_type=F32
        )

    hidden_grads = lax.fori_loop(0, 8, project, jnp.zeros((TOKENS, 2 * UNITS), F32), unroll=2)
    for core, (small_ref, start) in enumerate(((near_ref, 0), (away_ref, WIDTH))):
        hidden_grad = hidden_grads[:, core * UNITS : (core + 1) * UNITS]
        gate, upper = both_ref[core, :, :UNITS], both_ref[core, :, UNITS:]
        sigmoid_gate = jax.nn.sigmoid(gate)
        gate_cot = hidden_grad * upper * sigmoid_gate * (1.0 + gate * (1.0 - sigmoid_gate))
        up_cot = hidden_grad * (gate * sigmoid_gate)
        cots = jnp.concatenate([gate_cot, up_cot], axis=1).astype(BF16)
        back_ref[core] = cots
        small_ref[:, start : start + UNITS] = hidden_ref[:, core * UNITS : (core + 1) * UNITS]
        small_ref[:, start + UNITS : start + TRIPLE] = cots

    def outward(step, carry):
        cols = span(step, 512)
        values = sum(
            lax.dot_general(back_ref[core], wide_ref[cols, :], NT, preferred_element_type=F32)
            for core, wide_ref in enumerate(wides)
        )
        put(first_ref, moved, cols, values)
        away_ref[:, cols] = joined(pieces, cols)
        return carry

    lax.fori_loop(0, 16, outward, 0, unroll=2)


def turned(values):
    return jnp.concatenate(values, axis=0).astype(F32).T.astype(BF16)


def down_grad_kernel(*refs):
    pieces = (*refs[:4], refs[5])
    near_ref, away_ref, select_ref, keep_ref, send_ref, strip_ref = refs[4:]
    hidden = turned([near_ref[:, :UNITS], away_ref[:, WIDTH : WIDTH + UNITS]])

    def dense(step, carry):
        values = jnp.dot(
            hidden, joined(pieces, span(step, 512)), preferred_element_type=F32
        )
        for part in range(4):
            for unit in range(2):
                strip_ref[unit, pl.ds(step * 4 + part, SIDE, SIDE), :] = values[
                    unit * SIDE : (unit + 1) * SIDE, part * LANES : (part + 1) * LANES
                ]
        return carry

    lax.fori_loop(0, 16, dense, 0, unroll=2)

    def pick(step, carry):
        cols = span(step, 256)
        rows = jnp.concatenate([strip_ref[0, cols, :], strip_ref[1, cols, :]], axis=1)
        values = lax.dot_general(
            select_ref[...], rows.astype(BF16), NT, preferred_element_type=F32
        ).astype(BF16)
        keep_ref[:, cols] = values[:KEPT]
        send_ref[:, cols] = values[KEPT:]
        return carry

    lax.fori_loop(0, 16, pick, 0, unroll=2)


def paired(total_ref, cols, values):
    for entry in range(HALF):
        total_ref[entry, :, cols] = values[2 * entry : 2 * entry + 2]


def wide_grad_kernel(*refs):
    pieces = refs[:8]
    here_ref, far_ref, select_ref, gate_ref, up_ref, total_ref, done = refs[8:]
    cots = turned([here_ref[:, UNITS:], far_ref[:, UNITS:]])

    def step_of(step, carry):
        values = jnp.dot(
            cots, joined(pieces, span(step, 512)), preferred_element_type=F32
        ).astype(BF16)
        for matrix in range(2):
            rows = jnp.concatenate(
                [
                    jnp.concatenate(
                        [
                            values[
                                matrix * UNITS + unit * SIDE : matrix * UNITS + (unit + 1) * SIDE,
                                part * LANES : (part + 1) * LANES,
                            ]
                            for unit in range(2)
                        ],
                        axis=1,
                    )
                    for part in range(4)
                ],
                axis=0,
            )
            picked = lax.dot_general(select_ref[matrix], rows, NT, preferred_element_type=F32)
            paired(total_ref.at[matrix], span(step, 256), picked)
        return carry

    lax.fori_loop(0, 16, step_of, 0, unroll=2)
    copies = [
        pltpu.make_async_copy(total_ref.at[place], out_ref, done.at[place])
        for place, out_ref in enumerate((gate_ref, up_ref))
    ]
    for copy in copies:
        copy.start()
    for copy in copies:
        copy.wait()


def settle_kernel(keep_ref, send_ref, out_ref, total_ref, done):
    def settle(step, carry):
        cols = span(step, 512)
        paired(total_ref, cols, keep_ref[:, cols].astype(F32) + send_ref[:, cols].astype(F32))
        return carry

    lax.fori_loop(0, 8, settle, 0)
    copy = pltpu.make_async_copy(total_ref, out_ref, done)
    copy.start()
    copy.wait()


def ring(size, shift):
    return [(place, (place + shift) % size) for place in range(size)]


def per_device(
    activations, out_cotangent, gate_blocks, up_blocks, down_blocks, block_index, block_counts
):
    length = gate_blocks.shape[1]
    def shaped(dims, kind=BF16):
        return jax.ShapeDtypeStruct(dims, kind)

    def along(first):
        return [first] + [lax.ppermute(first, "y", ring(4, shift)) for shift in SHIFTS]

    def over(piece):
        return lax.ppermute(piece, "c", ring(2, 1))

    def swap(piece):
        return lax.ppermute(piece, "rep", ring(2, 1))

    def back(moved):
        return [
            lax.ppermute(part, "y", ring(4, -shift)) for part, shift in zip(moved, SHIFTS)
        ]

    def collect(first, moved):
        return (first + sum(part.astype(F32) for part in moved)).astype(BF16)

    tie = lax.optimization_barrier
    rows = jnp.stack([activations, out_cotangent], axis=1).reshape(1, 2, LANES, SIDE)
    rows = jnp.broadcast_to(jnp.swapaxes(rows, 2, 3), (FAR, 2, SIDE, LANES))
    rows = lax.all_to_all(rows, ("xh", "z"), 0, 0, tiled=True).reshape(FAR, 2, WIDTH)
    act_first, cot_first = rows[:, 0], rows[:, 1]

    live = jnp.arange(length)[None, None, :] < block_counts[:, :, None]
    places = jnp.where(live, block_index, -1)
    pick = (places[:, :, None, :] == jnp.arange(LANES)[None, None, :, None]).astype(BF16)
    pick = pick.reshape(6, LANES, length)
    wide = call(
        densify_wide_kernel,
        [shaped((WIDTH, 2 * UNITS))],
        [],
        3,
        pick[:4],
        gate_blocks,
        up_blocks,
    )[0]
    down = call(
        densify_down_kernel,
        [shaped((UNITS, WIDTH))],
        [pltpu.VMEM((2, SIDE * SIDE, LANES), F32)],
        8,
        pick,
        down_blocks,
    )[0]
    act_first, cot_first, wide, down, places = tie((act_first, cot_first, wide, down, places))

    acts = along(act_first)
    wides, downs = (wide, over(wide)), (down, over(down))
    halves = places.reshape(3, 2, 2, HALF)
    halves = jnp.where(lax.axis_index("rep") == 0, halves, halves[:, :, ::-1])
    halves = jnp.transpose(halves, (0, 2, 3, 1))
    goal = jnp.where(halves >= 0, halves + LANES * jnp.arange(2), -1)
    select = (goal.reshape(3, 2 * KEPT)[:, :, None] == jnp.arange(2 * LANES)).astype(BF16)
    acts, wides, downs, cot_first, select = tie((acts, wides, downs, cot_first, select))

    cot_pieces = along(cot_first)
    first, moved = shaped((ROWS, WIDTH), F32), [shaped((ROWS, WIDTH))] * 3
    lump = shaped((2 * ROWS, WIDTH))
    both, hidden, low, high, out_first, *out_moved = call(
        forward_kernel,
        [
            shaped((2, TOKENS, 2 * UNITS), F32),
            shaped((TOKENS, 2 * UNITS)),
            lump,
            lump,
            first,
            *moved,
        ],
        [],
        4,
        *acts,
        *wides,
        *downs,
    )
    cot_pieces, both, hidden, low, high, out_moved = tie(
        (cot_pieces, both, hidden, low, high, out_moved)
    )

    out_moved = back(out_moved)
    far_low = swap(low)
    over_low = over(low)
    near, away, grad_first, *grad_moved = call(
        backward_kernel,
        [shaped((TOKENS, TRIPLE)), shaped((TOKENS, WIDTH + TRIPLE)), first, *moved],
        [pltpu.VMEM((2, TOKENS, 2 * UNITS), BF16)],
        4,
        *cot_pieces,
        *wides,
        *downs,
        both,
        hidden,
    )
    out_moved, far_low, over_low, near, away, grad_moved, high = tie(
        (out_moved, far_low, over_low, near, away, grad_moved, high)
    )

    grad_moved = back(grad_moved)
    far_high = swap(high)
    away = over(away)
    here = jnp.concatenate([near, away[:, WIDTH:]], axis=0)
    far = swap(here)
    kept = sent = shaped((KEPT, SIDE * SIDE))
    keep_down, send_down = call(
        down_grad_kernel,
        [kept, sent],
        [pltpu.VMEM((2, SIDE * SIDE, LANES), F32)],
        7,
        *cot_pieces,
        near,
        away,
        select[2],
    )
    send_down, grad_moved, here, far, far_high = tie(
        (send_down, grad_moved, here, far, far_high)
    )

    come_down = swap(send_down)
    acts = [low, high, over_low, over(high), far_low, far_high, over(far_low), over(far_high)]
    total = jnp.stack([collect(out_first, out_moved), collect(grad_first, grad_moved)], axis=1)
    total = lax.all_to_all(
        total.reshape(FAR, 2, SIDE, LANES), ("xh", "z"), 0, 0, tiled=True
    )
    grad = shaped((HALF, 2, SIDE * SIDE), F32)
    gate_grad, up_grad = call(
        wide_grad_kernel,
        [grad, grad],
        [pltpu.VMEM((2, HALF, 2, SIDE * SIDE), F32), pltpu.SemaphoreType.DMA((2,))],
        7,
        *acts,
        here,
        far,
        select[:2, :KEPT],
        space=pltpu.HBM,
    )
    down_grad = call(
        settle_kernel,
        [grad],
        [pltpu.VMEM((HALF, 2, SIDE * SIDE), F32), pltpu.SemaphoreType.DMA],
        1.5,
        keep_down,
        come_down,
        space=pltpu.HBM,
    )[0]
    gate_grad, up_grad, down_grad = (
        jnp.swapaxes(grad, 0, 1) for grad in (gate_grad, up_grad, down_grad)
    )
    total = jnp.sum(total.astype(F32), axis=0)
    total = jnp.swapaxes(total, 1, 2).reshape(2, 1, WIDTH).astype(BF16)
    return (total[0], total[1], gate_grad, up_grad, down_grad)


def solution(mesh):
    fine = Mesh(mesh.devices.reshape(2, 8, 4, 2, 2), ("xh", "z", "y", "c", "rep"))
    blk = ("xh", "z", "y", "c")
    placed = (
        P((*blk, "rep"), None),
        P((*blk, "rep"), None),
        P(blk, None, None),
        P(blk, None, None),
        P(blk, None, None),
        P(None, blk, None),
        P(None, blk),
    )
    return jax.shard_map(
        per_device,
        mesh=fine,
        in_specs=placed,
        out_specs=(
            P((*blk, "rep"), None),
            P((*blk, "rep"), None),
            P(blk, "rep", None),
            P(blk, "rep", None),
            P(blk, "rep", None),
        ),
        check_vma=False,
    )
```

```python
import functools

import jax
import jax.numpy as jnp
from jax import lax
from jax.experimental import pallas as pl
from jax.experimental.pallas import tpu as pltpu
from jax.sharding import Mesh
from jax.sharding import PartitionSpec as P

SIDE = 64
LANES = 128
WIDTH = SIDE * LANES
UNITS = 2 * SIDE
TRIPLE = 3 * UNITS
HALF = 36
KEPT = 2 * HALF
ROWS = 16
TOKENS = 4 * ROWS
FAR = 16
SHIFTS = (2, 1, 3)
VMEM_BYTES = 14 * 1024 * 1024
SMALL_BYTES = 8 * 1024 * 1024
BF16 = jnp.bfloat16
F32 = jnp.float32
NT = (((1,), (1,)), ((), ()))


def call(kernel, outs, scratch, *operands, inside=(), space=pltpu.VMEM, limit=VMEM_BYTES):
    inside = dict(inside)
    return pl.pallas_call(
        kernel,
        out_shape=outs,
        in_specs=[
            pl.BlockSpec(memory_space=inside.get(place, pltpu.VMEM))
            for place in range(len(operands))
        ],
        out_specs=[pl.BlockSpec(memory_space=space)] * len(outs),
        scratch_shapes=scratch,
        compiler_params=pltpu.CompilerParams(vmem_limit_bytes=limit),
        cost_estimate=pl.CostEstimate(flops=0, bytes_accessed=100_000, transcendentals=0),
    )(*operands)


def span(step, width):
    return pl.ds(pl.multiple_of(step * width, width), width)


def spread_kernel(act_ref, cot_ref, out_ref, strip_ref):
    for which, row_ref in enumerate((act_ref, cot_ref)):
        row = row_ref[...].astype(F32)
        for part in range(SIDE):
            strip_ref[part : part + 1, :] = row[:, part * LANES : (part + 1) * LANES]
        turned_row = strip_ref[...].T
        tile = jnp.concatenate([turned_row[:SIDE], turned_row[SIDE:]], axis=1).astype(BF16)
        for place in range(FAR):
            out_ref[place, which] = tile


def gather_kernel(tiles_ref, act_ref, cot_ref, strip_ref):
    for which, out_ref in enumerate((act_ref, cot_ref)):
        for place in range(FAR):
            strip_ref[which, place * SIDE : (place + 1) * SIDE, :] = tiles_ref[
                place, which
            ].astype(F32)
        for inner in range(SIDE):
            out_ref[:, inner * LANES : (inner + 1) * LANES] = strip_ref[
                which, pl.ds(inner, FAR, SIDE), :
            ].astype(BF16)


def collect_kernel(*refs):
    *parts, tiles_ref, strip_ref = refs
    for which in range(2):
        first_ref, *moved = parts[4 * which : 4 * which + 4]
        for inner in range(SIDE):
            cols = slice(inner * LANES, (inner + 1) * LANES)
            total = first_ref[:, cols]
            for ref in moved:
                total = total + ref[:, cols].astype(F32)
            strip_ref[which, pl.ds(inner, FAR, SIDE), :] = total
        for place in range(FAR):
            tiles_ref[place, which] = strip_ref[
                which, place * SIDE : (place + 1) * SIDE, :
            ].astype(BF16)


def finish_kernel(total_ref, out_ref, grad_ref, strip_ref):
    for which, row_ref in enumerate((out_ref, grad_ref)):
        total = total_ref[0, which].astype(F32)
        for place in range(1, FAR):
            total = total + total_ref[place, which].astype(F32)
        strip_ref[...] = jnp.concatenate([total[:, :SIDE], total[:, SIDE:]], axis=0).T
        for part in range(SIDE):
            row_ref[:, part * LANES : (part + 1) * LANES] = strip_ref[
                part : part + 1, :
            ].astype(BF16)


def lane_of(block):
    return (block & 1) * SIDE + (block >> 1)


def one_hot(index_ref, count_ref, matrix, unit):
    entries = index_ref[matrix, unit : unit + 1, :]
    shape = (LANES, entries.shape[1])
    rows = lax.broadcasted_iota(jnp.int32, shape, 0)
    live = lax.broadcasted_iota(jnp.int32, shape, 1) < count_ref[matrix, unit]
    return jnp.where((rows == lane_of(entries)) & live, 1.0, 0.0).astype(BF16)


def densify_wide_kernel(index_ref, count_ref, gate_ref, up_ref, wide_ref):
    picks = [[one_hot(index_ref, count_ref, matrix, unit) for unit in range(2)] for matrix in range(2)]

    def spread(step, carry):
        cols = span(step, 4 * SIDE)
        for matrix, blocks_ref in enumerate((gate_ref, up_ref)):
            first, second = (
                jnp.dot(
                    picks[matrix][unit],
                    blocks_ref[unit, :, cols],
                    preferred_element_type=F32,
                ).astype(BF16)
                for unit in range(2)
            )
            for inner in range(4):
                part = slice(inner * SIDE, (inner + 1) * SIDE)
                wide_ref[
                    span(step * 4 + inner, LANES), matrix * UNITS : (matrix + 1) * UNITS
                ] = jnp.concatenate([first[:, part], second[:, part]], axis=1)
        return carry

    lax.fori_loop(0, 16, spread, 0, unroll=2)


def densify_down_kernel(index_ref, count_ref, down_ref, dense_ref, strip_ref):
    for unit in range(2):
        pick = one_hot(index_ref, count_ref, 2, unit)

        def turn(step, carry, unit=unit, pick=pick):
            dense = jnp.dot(
                pick,
                down_ref[unit, :, span(step, 256)],
                preferred_element_type=F32,
            )
            strip_ref[unit, span(step, 256), :] = dense.T
            return carry

        lax.fori_loop(0, 16, turn, 0, unroll=2)

    def gather(inner, carry):
        dense_ref[:, span(inner, LANES)] = jnp.concatenate(
            [strip_ref[unit, pl.ds(inner, SIDE, SIDE), :] for unit in range(2)], axis=0
        ).astype(BF16)
        return carry

    lax.fori_loop(0, SIDE, gather, 0, unroll=8)


def joined(pieces, cols):
    return jnp.concatenate([piece[:, cols] for piece in pieces], axis=0)


def put(first_ref, moved, cols, values):
    first_ref[:, cols] = values[:ROWS]
    for slot, ref in enumerate(moved):
        ref[:, cols] = values[(slot + 1) * ROWS : (slot + 2) * ROWS].astype(BF16)


def forward_kernel(*refs):
    pieces = refs[:4]
    wides, downs = refs[4:6], refs[6:8]
    both_ref, hidden_ref, low_ref, high_ref, first_ref, *moved = refs[8:]

    def project(step, totals):
        cols = span(step, 1024)
        rows = joined(pieces, cols)
        return tuple(
            total + jnp.dot(rows, wide_ref[cols, :], preferred_element_type=F32)
            for total, wide_ref in zip(totals, wides)
        )

    zeros = jnp.zeros((TOKENS, 2 * UNITS), F32)
    totals = lax.fori_loop(0, 8, project, (zeros, zeros), unroll=2)
    hidden = []
    for core, both in enumerate(totals):
        both_ref[core] = both
        gate, upper = both[:, :UNITS], both[:, UNITS:]
        hidden.append((gate * jax.nn.sigmoid(gate) * upper).astype(BF16))
    hidden = jnp.concatenate(hidden, axis=1)
    hidden_ref[...] = hidden

    def outward(step, carry):
        cols = span(step, 512)
        weights = jnp.concatenate([down_ref[:, cols] for down_ref in downs], axis=0)
        put(first_ref, moved, cols, jnp.dot(hidden, weights, preferred_element_type=F32))
        low_ref[:, cols] = joined(pieces[:2], cols)
        high_ref[:, cols] = joined(pieces[2:], cols)
        return carry

    lax.fori_loop(0, 16, outward, 0, unroll=2)


def backward_kernel(*refs):
    pieces = refs[:4]
    wides, downs = refs[4:6], refs[6:8]
    both_ref, hidden_ref, near_ref, away_ref, first_ref, *moved, back_ref = refs[8:]

    def project(step, total):
        cols = span(step, 1024)
        weights = jnp.concatenate([down_ref[:, cols] for down_ref in downs], axis=0)
        return total + lax.dot_general(
            joined(pieces, cols), weights, NT, preferred_element_type=F32
        )

    hidden_grads = lax.fori_loop(0, 8, project, jnp.zeros((TOKENS, 2 * UNITS), F32), unroll=2)
    for core, (small_ref, start) in enumerate(((near_ref, 0), (away_ref, WIDTH))):
        hidden_grad = hidden_grads[:, core * UNITS : (core + 1) * UNITS]
        gate, upper = both_ref[core, :, :UNITS], both_ref[core, :, UNITS:]
        sigmoid_gate = jax.nn.sigmoid(gate)
        gate_cot = hidden_grad * upper * sigmoid_gate * (1.0 + gate * (1.0 - sigmoid_gate))
        up_cot = hidden_grad * (gate * sigmoid_gate)
        cots = jnp.concatenate([gate_cot, up_cot], axis=1).astype(BF16)
        back_ref[core] = cots
        small_ref[:, start : start + UNITS] = hidden_ref[:, core * UNITS : (core + 1) * UNITS]
        small_ref[:, start + UNITS : start + TRIPLE] = cots

    def outward(step, carry):
        cols = span(step, 512)
        values = sum(
            lax.dot_general(back_ref[core], wide_ref[cols, :], NT, preferred_element_type=F32)
            for core, wide_ref in enumerate(wides)
        )
        put(first_ref, moved, cols, values)
        away_ref[:, cols] = joined(pieces, cols)
        return carry

    lax.fori_loop(0, 16, outward, 0, unroll=2)


def turned(values):
    return jnp.concatenate(values, axis=0).astype(F32).T.astype(BF16)


def down_grad_kernel(*refs):
    pieces = (*refs[:4], refs[5])
    near_ref, away_ref, select_ref, keep_ref, send_ref, strip_ref = refs[4:]
    hidden = turned([near_ref[:, :UNITS], away_ref[:, WIDTH : WIDTH + UNITS]])

    def dense(step, carry):
        values = jnp.dot(
            hidden, joined(pieces, span(step, 512)), preferred_element_type=F32
        )
        for part in range(4):
            for unit in range(2):
                strip_ref[unit, pl.ds(step * 4 + part, SIDE, SIDE), :] = values[
                    unit * SIDE : (unit + 1) * SIDE, part * LANES : (part + 1) * LANES
                ]
        return carry

    lax.fori_loop(0, 16, dense, 0, unroll=2)

    def pick(step, carry):
        cols = span(step, 256)
        rows = jnp.concatenate([strip_ref[0, cols, :], strip_ref[1, cols, :]], axis=1)
        values = lax.dot_general(
            select_ref[...], rows.astype(BF16), NT, preferred_element_type=F32
        ).astype(BF16)
        keep_ref[:, cols] = values[:KEPT]
        send_ref[:, cols] = values[KEPT:]
        return carry

    lax.fori_loop(0, 16, pick, 0, unroll=2)


def paired(total_ref, cols, values):
    for entry in range(HALF):
        total_ref[entry, :, cols] = values[2 * entry : 2 * entry + 2]


def wide_grad_kernel(*refs):
    pieces = refs[:8]
    here_ref, far_ref, select_ref, gate_ref, up_ref, total_ref, done = refs[8:]
    cots = turned([here_ref[:, UNITS:], far_ref[:, UNITS:]])

    def step_of(step, carry):
        values = jnp.dot(
            cots, joined(pieces, span(step, 512)), preferred_element_type=F32
        ).astype(BF16)
        for matrix in range(2):
            rows = jnp.concatenate(
                [
                    jnp.concatenate(
                        [
                            values[
                                matrix * UNITS + unit * SIDE : matrix * UNITS + (unit + 1) * SIDE,
                                part * LANES : (part + 1) * LANES,
                            ]
                            for unit in range(2)
                        ],
                        axis=1,
                    )
                    for part in range(4)
                ],
                axis=0,
            )
            picked = lax.dot_general(select_ref[matrix], rows, NT, preferred_element_type=F32)
            paired(total_ref.at[matrix], span(step, 256), picked)
        return carry

    lax.fori_loop(0, 16, step_of, 0, unroll=2)
    copies = [
        pltpu.make_async_copy(total_ref.at[place], out_ref, done.at[place])
        for place, out_ref in enumerate((gate_ref, up_ref))
    ]
    for copy in copies:
        copy.start()
    for copy in copies:
        copy.wait()


def settle_kernel(keep_ref, send_ref, out_ref, total_ref, done):
    def settle(step, carry):
        cols = span(step, 512)
        paired(total_ref, cols, keep_ref[:, cols].astype(F32) + send_ref[:, cols].astype(F32))
        return carry

    lax.fori_loop(0, 8, settle, 0)
    copy = pltpu.make_async_copy(total_ref, out_ref, done)
    copy.start()
    copy.wait()


def ring(size, shift):
    return [(place, (place + shift) % size) for place in range(size)]


def per_device(
    activations, out_cotangent, gate_blocks, up_blocks, down_blocks, block_index, block_counts
):
    length = gate_blocks.shape[1]
    def shaped(dims, kind=BF16):
        return jax.ShapeDtypeStruct(dims, kind)

    def along(first):
        return [first] + [lax.ppermute(first, "y", ring(4, shift)) for shift in SHIFTS]

    def over(piece):
        return lax.ppermute(piece, "c", ring(2, 1))

    def swap(piece):
        return lax.ppermute(piece, "rep", ring(2, 1))

    def back(moved):
        return [
            lax.ppermute(part, "y", ring(4, -shift)) for part, shift in zip(moved, SHIFTS)
        ]

    tie = lax.optimization_barrier
    numbers = (block_index, block_counts)
    strips = pltpu.VMEM((2, SIDE * FAR, LANES), F32)

    def exchange(tiles):
        return lax.all_to_all(tiles, ("xh", "z"), 0, 0, tiled=True)

    tiles = call(
        spread_kernel,
        [shaped((FAR, 2, SIDE, LANES))],
        [pltpu.VMEM((SIDE, LANES), F32)],
        activations,
        out_cotangent,
        limit=SMALL_BYTES,
    )[0]
    tiles = exchange(tiles)
    down = call(
        densify_down_kernel,
        [shaped((UNITS, WIDTH))],
        [pltpu.VMEM((2, SIDE * SIDE, LANES), F32)],
        *numbers,
        down_blocks,
        inside={1: pltpu.SMEM},
    )[0]
    wide = call(
        densify_wide_kernel,
        [shaped((WIDTH, 2 * UNITS))],
        [],
        *numbers,
        gate_blocks,
        up_blocks,
        inside={1: pltpu.SMEM},
    )[0]
    tiles, wide, down, block_index = tie((tiles, wide, down, block_index))
    act_first, cot_first = call(
        gather_kernel, [shaped((ROWS, WIDTH))] * 2, [strips], tiles, limit=SMALL_BYTES
    )
    acts = along(act_first)
    wides, downs = (wide, over(wide)), (down, over(down))
    live = jnp.arange(length)[None, None, :] < block_counts[:, :, None]
    places = jnp.where(live, lane_of(block_index), -1)
    halves = places.reshape(3, 2, 2, HALF)
    halves = jnp.where(lax.axis_index("rep") == 0, halves, halves[:, :, ::-1])
    halves = jnp.transpose(halves, (0, 2, 3, 1))
    goal = jnp.where(halves >= 0, halves + LANES * jnp.arange(2), -1)
    select = (goal.reshape(3, 2 * KEPT)[:, :, None] == jnp.arange(2 * LANES)).astype(BF16)

    cot_pieces = along(cot_first)
    first, moved = shaped((ROWS, WIDTH), F32), [shaped((ROWS, WIDTH))] * 3
    lump = shaped((2 * ROWS, WIDTH))
    both, hidden, low, high, out_first, *out_moved = call(
        forward_kernel,
        [
            shaped((2, TOKENS, 2 * UNITS), F32),
            shaped((TOKENS, 2 * UNITS)),
            lump,
            lump,
            first,
            *moved,
        ],
        [],
        *acts,
        *wides,
        *downs,
    )
    cot_pieces, both, hidden, low, high, out_moved = tie(
        (cot_pieces, both, hidden, low, high, out_moved)
    )

    out_moved = back(out_moved)
    far_low = swap(low)
    near, away, grad_first, *grad_moved = call(
        backward_kernel,
        [shaped((TOKENS, TRIPLE)), shaped((TOKENS, WIDTH + TRIPLE)), first, *moved],
        [pltpu.VMEM((2, TOKENS, 2 * UNITS), BF16)],
        *cot_pieces,
        *wides,
        *downs,
        both,
        hidden,
    )
    out_moved, far_low, near, away, high = tie((out_moved, far_low, near, away, high))

    grad_moved = back(grad_moved)
    far_high = swap(high)
    away = over(away)
    here = jnp.concatenate([near, away[:, WIDTH:]], axis=0)
    far = swap(here)
    kept = sent = shaped((KEPT, SIDE * SIDE))
    keep_down, send_down = call(
        down_grad_kernel,
        [kept, sent],
        [pltpu.VMEM((2, SIDE * SIDE, LANES), F32)],
        *cot_pieces,
        near,
        away,
        select[2],
    )
    send_down, grad_moved, here, far, far_high = tie(
        (send_down, grad_moved, here, far, far_high)
    )

    come_down = swap(send_down)
    acts = [low, high, over(low), over(high), far_low, far_high, over(far_low), over(far_high)]
    tiles = exchange(
        call(
            collect_kernel,
            [shaped((FAR, 2, SIDE, LANES))],
            [strips],
            out_first,
            *out_moved,
            grad_first,
            *grad_moved,
            limit=SMALL_BYTES,
        )[0]
    )
    grad = shaped((HALF, 2, SIDE * SIDE), F32)
    gate_grad, up_grad = call(
        wide_grad_kernel,
        [grad, grad],
        [pltpu.VMEM((2, HALF, 2, SIDE * SIDE), F32), pltpu.SemaphoreType.DMA((2,))],
        *acts,
        here,
        far,
        select[:2, :KEPT],
        space=pltpu.HBM,
    )
    down_grad = call(
        settle_kernel,
        [grad],
        [pltpu.VMEM((HALF, 2, SIDE * SIDE), F32), pltpu.SemaphoreType.DMA],
        keep_down,
        come_down,
        space=pltpu.HBM,
    )[0]
    gate_grad, up_grad, down_grad = (
        jnp.swapaxes(grad, 0, 1) for grad in (gate_grad, up_grad, down_grad)
    )
    layer_out, input_grad = call(
        finish_kernel,
        [shaped((1, WIDTH))] * 2,
        [pltpu.VMEM((SIDE, LANES), F32)],
        tiles,
        limit=SMALL_BYTES,
    )
    return (layer_out, input_grad, gate_grad, up_grad, down_grad)


def solution(mesh):
    fine = Mesh(mesh.devices.reshape(2, 8, 4, 2, 2), ("xh", "z", "y", "c", "rep"))
    blk = ("xh", "z", "y", "c")
    placed = (
        P((*blk, "rep"), None),
        P((*blk, "rep"), None),
        P(blk, None, None),
        P(blk, None, None),
        P(blk, None, None),
        P(None, blk, None),
        P(None, blk),
    )
    return jax.shard_map(
        per_device,
        mesh=fine,
        in_specs=placed,
        out_specs=(
            P((*blk, "rep"), None),
            P((*blk, "rep"), None),
            P(blk, "rep", None),
            P(blk, "rep", None),
            P(blk, "rep", None),
        ),
        check_vma=False,
    )
```

```python
import functools

import jax
import jax.numpy as jnp
from jax import lax
from jax.experimental import pallas as pl
from jax.experimental.pallas import tpu as pltpu
from jax.sharding import Mesh
from jax.sharding import PartitionSpec as P

SIDE = 64
LANES = 128
WIDTH = SIDE * LANES
UNITS = 2 * SIDE
TRIPLE = 3 * UNITS
HALF = 36
KEPT = 2 * HALF
ROWS = 16
TOKENS = 4 * ROWS
FAR = 16
SHIFTS = (2, 1, 3)
VMEM_BYTES = 14 * 1024 * 1024
SMALL_BYTES = 8 * 1024 * 1024
BF16 = jnp.bfloat16
F32 = jnp.float32
NT = (((1,), (1,)), ((), ()))


def call(kernel, outs, scratch, *operands, inside=(), space=pltpu.VMEM, limit=VMEM_BYTES):
    inside = dict(inside)
    return pl.pallas_call(
        kernel,
        out_shape=outs,
        in_specs=[
            pl.BlockSpec(memory_space=inside.get(place, pltpu.VMEM))
            for place in range(len(operands))
        ],
        out_specs=[pl.BlockSpec(memory_space=space)] * len(outs),
        scratch_shapes=scratch,
        compiler_params=pltpu.CompilerParams(vmem_limit_bytes=limit),
        cost_estimate=pl.CostEstimate(flops=0, bytes_accessed=100_000, transcendentals=0),
    )(*operands)


def span(step, width):
    return pl.ds(pl.multiple_of(step * width, width), width)


def spread_kernel(act_ref, cot_ref, out_ref, strip_ref):
    for which, row_ref in enumerate((act_ref, cot_ref)):
        row = row_ref[...].astype(F32)
        for part in range(SIDE):
            strip_ref[part : part + 1, :] = row[:, part * LANES : (part + 1) * LANES]
        turned_row = strip_ref[...].T
        tile = jnp.concatenate([turned_row[:SIDE], turned_row[SIDE:]], axis=1).astype(BF16)
        for place in range(FAR):
            out_ref[place, which] = tile


def gather_kernel(tiles_ref, act_ref, cot_ref, strip_ref):
    for which, out_ref in enumerate((act_ref, cot_ref)):
        for place in range(FAR):
            strip_ref[which, place * SIDE : (place + 1) * SIDE, :] = tiles_ref[
                place, which
            ].astype(F32)
        for inner in range(SIDE):
            out_ref[:, inner * LANES : (inner + 1) * LANES] = strip_ref[
                which, pl.ds(inner, FAR, SIDE), :
            ].astype(BF16)


def summed(first_ref, moved, strip_ref, tiles_ref):
    for inner in range(SIDE):
        cols = slice(inner * LANES, (inner + 1) * LANES)
        total = first_ref[:, cols]
        for ref in moved:
            total = total + ref[:, cols].astype(F32)
        strip_ref[pl.ds(inner, FAR, SIDE), :] = total
    for place in range(FAR):
        tiles_ref[place] = strip_ref[place * SIDE : (place + 1) * SIDE, :].astype(BF16)


def collect_kernel(first_ref, *refs):
    *moved, tiles_ref, strip_ref = refs
    summed(first_ref, moved, strip_ref, tiles_ref)


def join_kernel(out_ref, first_ref, *refs):
    *moved, tiles_ref, strip_ref = refs
    tiles_ref[:, 0] = out_ref[...]
    summed(first_ref, moved, strip_ref, tiles_ref.at[:, 1])


def finish_kernel(total_ref, out_ref, grad_ref, strip_ref):
    for which, row_ref in enumerate((out_ref, grad_ref)):
        total = total_ref[0, which].astype(F32)
        for place in range(1, FAR):
            total = total + total_ref[place, which].astype(F32)
        strip_ref[...] = jnp.concatenate([total[:, :SIDE], total[:, SIDE:]], axis=0).T
        for part in range(SIDE):
            row_ref[:, part * LANES : (part + 1) * LANES] = strip_ref[
                part : part + 1, :
            ].astype(BF16)


def lane_of(block):
    return (block & 1) * SIDE + (block >> 1)


def one_hot(index_ref, count_ref, matrix, unit):
    entries = index_ref[matrix, unit : unit + 1, :]
    shape = (LANES, entries.shape[1])
    rows = lax.broadcasted_iota(jnp.int32, shape, 0)
    live = lax.broadcasted_iota(jnp.int32, shape, 1) < count_ref[matrix, unit]
    return jnp.where((rows == lane_of(entries)) & live, 1.0, 0.0).astype(BF16)


def densify_wide_kernel(index_ref, count_ref, gate_ref, up_ref, wide_ref):
    picks = [[one_hot(index_ref, count_ref, matrix, unit) for unit in range(2)] for matrix in range(2)]

    def spread(step, carry):
        cols = span(step, 4 * SIDE)
        for matrix, blocks_ref in enumerate((gate_ref, up_ref)):
            first, second = (
                jnp.dot(
                    picks[matrix][unit],
                    blocks_ref[unit, :, cols],
                    preferred_element_type=F32,
                ).astype(BF16)
                for unit in range(2)
            )
            for inner in range(4):
                part = slice(inner * SIDE, (inner + 1) * SIDE)
                wide_ref[
                    span(step * 4 + inner, LANES), matrix * UNITS : (matrix + 1) * UNITS
                ] = jnp.concatenate([first[:, part], second[:, part]], axis=1)
        return carry

    lax.fori_loop(0, 16, spread, 0, unroll=2)


def densify_down_kernel(index_ref, count_ref, down_ref, dense_ref, strip_ref):
    for unit in range(2):
        pick = one_hot(index_ref, count_ref, 2, unit)

        def turn(step, carry, unit=unit, pick=pick):
            dense = jnp.dot(
                pick,
                down_ref[unit, :, span(step, 256)],
                preferred_element_type=F32,
            )
            strip_ref[unit, span(step, 256), :] = dense.T
            return carry

        lax.fori_loop(0, 16, turn, 0, unroll=2)

    def gather(inner, carry):
        dense_ref[:, span(inner, LANES)] = jnp.concatenate(
            [strip_ref[unit, pl.ds(inner, SIDE, SIDE), :] for unit in range(2)], axis=0
        ).astype(BF16)
        return carry

    lax.fori_loop(0, SIDE, gather, 0, unroll=8)


def joined(pieces, cols):
    return jnp.concatenate([piece[:, cols] for piece in pieces], axis=0)


def put(first_ref, moved, cols, values):
    first_ref[:, cols] = values[:ROWS]
    for slot, ref in enumerate(moved):
        ref[:, cols] = values[(slot + 1) * ROWS : (slot + 2) * ROWS].astype(BF16)


def forward_kernel(*refs):
    pieces = refs[:4]
    wides, downs = refs[4:6], refs[6:8]
    both_ref, hidden_ref, low_ref, high_ref, first_ref, *moved = refs[8:]

    def project(step, totals):
        cols = span(step, 1024)
        rows = joined(pieces, cols)
        return tuple(
            total + jnp.dot(rows, wide_ref[cols, :], preferred_element_type=F32)
            for total, wide_ref in zip(totals, wides)
        )

    zeros = jnp.zeros((TOKENS, 2 * UNITS), F32)
    totals = lax.fori_loop(0, 8, project, (zeros, zeros), unroll=2)
    hidden = []
    for core, both in enumerate(totals):
        both_ref[core] = both
        gate, upper = both[:, :UNITS], both[:, UNITS:]
        hidden.append((gate * jax.nn.sigmoid(gate) * upper).astype(BF16))
    hidden = jnp.concatenate(hidden, axis=1)
    hidden_ref[...] = hidden

    def outward(step, carry):
        cols = span(step, 512)
        weights = jnp.concatenate([down_ref[:, cols] for down_ref in downs], axis=0)
        put(first_ref, moved, cols, jnp.dot(hidden, weights, preferred_element_type=F32))
        low_ref[:, cols] = joined(pieces[:2], cols)
        high_ref[:, cols] = joined(pieces[2:], cols)
        return carry

    lax.fori_loop(0, 16, outward, 0, unroll=2)


def backward_kernel(*refs):
    pieces = refs[:4]
    wides, downs = refs[4:6], refs[6:8]
    both_ref, hidden_ref, near_ref, away_ref, first_ref, *moved, back_ref = refs[8:]

    def project(step, total):
        cols = span(step, 1024)
        weights = jnp.concatenate([down_ref[:, cols] for down_ref in downs], axis=0)
        return total + lax.dot_general(
            joined(pieces, cols), weights, NT, preferred_element_type=F32
        )

    hidden_grads = lax.fori_loop(0, 8, project, jnp.zeros((TOKENS, 2 * UNITS), F32), unroll=2)
    for core, (small_ref, start) in enumerate(((near_ref, 0), (away_ref, WIDTH))):
        hidden_grad = hidden_grads[:, core * UNITS : (core + 1) * UNITS]
        gate, upper = both_ref[core, :, :UNITS], both_ref[core, :, UNITS:]
        sigmoid_gate = jax.nn.sigmoid(gate)
        gate_cot = hidden_grad * upper * sigmoid_gate * (1.0 + gate * (1.0 - sigmoid_gate))
        up_cot = hidden_grad * (gate * sigmoid_gate)
        cots = jnp.concatenate([gate_cot, up_cot], axis=1).astype(BF16)
        back_ref[core] = cots
        small_ref[:, start : start + UNITS] = hidden_ref[:, core * UNITS : (core + 1) * UNITS]
        small_ref[:, start + UNITS : start + TRIPLE] = cots

    def outward(step, carry):
        cols = span(step, 512)
        values = sum(
            lax.dot_general(back_ref[core], wide_ref[cols, :], NT, preferred_element_type=F32)
            for core, wide_ref in enumerate(wides)
        )
        put(first_ref, moved, cols, values)
        away_ref[:, cols] = joined(pieces, cols)
        return carry

    lax.fori_loop(0, 16, outward, 0, unroll=2)


def turned(values):
    return jnp.concatenate(values, axis=0).astype(F32).T.astype(BF16)


def down_grad_kernel(*refs):
    pieces = (*refs[:4], refs[5])
    near_ref, away_ref, select_ref, keep_ref, send_ref, strip_ref = refs[4:]
    hidden = turned([near_ref[:, :UNITS], away_ref[:, WIDTH : WIDTH + UNITS]])

    def dense(step, carry):
        values = jnp.dot(
            hidden, joined(pieces, span(step, 512)), preferred_element_type=F32
        )
        for part in range(4):
            for unit in range(2):
                strip_ref[unit, pl.ds(step * 4 + part, SIDE, SIDE), :] = values[
                    unit * SIDE : (unit + 1) * SIDE, part * LANES : (part + 1) * LANES
                ]
        return carry

    lax.fori_loop(0, 16, dense, 0, unroll=2)

    def pick(step, carry):
        cols = span(step, 256)
        rows = jnp.concatenate([strip_ref[0, cols, :], strip_ref[1, cols, :]], axis=1)
        values = lax.dot_general(
            select_ref[...], rows.astype(BF16), NT, preferred_element_type=F32
        ).astype(BF16)
        keep_ref[:, cols] = values[:KEPT]
        send_ref[:, cols] = values[KEPT:]
        return carry

    lax.fori_loop(0, 16, pick, 0, unroll=2)


def paired(total_ref, cols, values):
    for entry in range(HALF):
        total_ref[entry, :, cols] = values[2 * entry : 2 * entry + 2]


def wide_grad_kernel(*refs):
    pieces = refs[:8]
    here_ref, far_ref, select_ref, gate_ref, up_ref, total_ref, done = refs[8:]
    cots = turned([here_ref[:, UNITS:], far_ref[:, UNITS:]])

    def step_of(step, carry):
        values = jnp.dot(
            cots, joined(pieces, span(step, 512)), preferred_element_type=F32
        ).astype(BF16)
        for matrix in range(2):
            rows = jnp.concatenate(
                [
                    jnp.concatenate(
                        [
                            values[
                                matrix * UNITS + unit * SIDE : matrix * UNITS + (unit + 1) * SIDE,
                                part * LANES : (part + 1) * LANES,
                            ]
                            for unit in range(2)
                        ],
                        axis=1,
                    )
                    for part in range(4)
                ],
                axis=0,
            )
            picked = lax.dot_general(select_ref[matrix], rows, NT, preferred_element_type=F32)
            paired(total_ref.at[matrix], span(step, 256), picked)
        return carry

    lax.fori_loop(0, 16, step_of, 0, unroll=2)
    copies = [
        pltpu.make_async_copy(total_ref.at[place], out_ref, done.at[place])
        for place, out_ref in enumerate((gate_ref, up_ref))
    ]
    for copy in copies:
        copy.start()
    for copy in copies:
        copy.wait()


def settle_kernel(keep_ref, send_ref, out_ref, total_ref, done):
    def settle(step, carry):
        cols = span(step, 512)
        paired(total_ref, cols, keep_ref[:, cols].astype(F32) + send_ref[:, cols].astype(F32))
        return carry

    lax.fori_loop(0, 8, settle, 0)
    copy = pltpu.make_async_copy(total_ref, out_ref, done)
    copy.start()
    copy.wait()


def ring(size, shift):
    return [(place, (place + shift) % size) for place in range(size)]


def per_device(
    activations, out_cotangent, gate_blocks, up_blocks, down_blocks, block_index, block_counts
):
    length = gate_blocks.shape[1]
    def shaped(dims, kind=BF16):
        return jax.ShapeDtypeStruct(dims, kind)

    def along(first):
        return [first] + [lax.ppermute(first, "y", ring(4, shift)) for shift in SHIFTS]

    def over(piece):
        return lax.ppermute(piece, "c", ring(2, 1))

    def swap(piece):
        return lax.ppermute(piece, "rep", ring(2, 1))

    def back(moved):
        return [
            lax.ppermute(part, "y", ring(4, -shift)) for part, shift in zip(moved, SHIFTS)
        ]

    tie = lax.optimization_barrier
    numbers = (block_index, block_counts)
    strips = pltpu.VMEM((2, SIDE * FAR, LANES), F32)
    strip = pltpu.VMEM((SIDE * FAR, LANES), F32)

    def exchange(tiles):
        return lax.all_to_all(tiles, ("xh", "z"), 0, 0, tiled=True)

    tiles = call(
        spread_kernel,
        [shaped((FAR, 2, SIDE, LANES))],
        [pltpu.VMEM((SIDE, LANES), F32)],
        activations,
        out_cotangent,
        limit=62 * 1024 * 1024,
    )[0]
    tiles = exchange(tiles)
    down = call(
        densify_down_kernel,
        [shaped((UNITS, WIDTH))],
        [pltpu.VMEM((2, SIDE * SIDE, LANES), F32)],
        *numbers,
        down_blocks,
        inside={1: pltpu.SMEM},
    )[0]
    wide = call(
        densify_wide_kernel,
        [shaped((WIDTH, 2 * UNITS))],
        [],
        *numbers,
        gate_blocks,
        up_blocks,
        inside={1: pltpu.SMEM},
    )[0]
    tiles, wide, down, block_index = tie((tiles, wide, down, block_index))
    act_first, cot_first = call(
        gather_kernel, [shaped((ROWS, WIDTH))] * 2, [strips], tiles, limit=SMALL_BYTES
    )
    acts = along(act_first)
    wides, downs = (wide, over(wide)), (down, over(down))
    live = jnp.arange(length)[None, None, :] < block_counts[:, :, None]
    places = jnp.where(live, lane_of(block_index), -1)
    halves = places.reshape(3, 2, 2, HALF)
    halves = jnp.where(lax.axis_index("rep") == 0, halves, halves[:, :, ::-1])
    halves = jnp.transpose(halves, (0, 2, 3, 1))
    goal = jnp.where(halves >= 0, halves + LANES * jnp.arange(2), -1)
    select = (goal.reshape(3, 2 * KEPT)[:, :, None] == jnp.arange(2 * LANES)).astype(BF16)

    cot_pieces = along(cot_first)
    first, moved = shaped((ROWS, WIDTH), F32), [shaped((ROWS, WIDTH))] * 3
    lump = shaped((2 * ROWS, WIDTH))
    both, hidden, low, high, out_first, *out_moved = call(
        forward_kernel,
        [
            shaped((2, TOKENS, 2 * UNITS), F32),
            shaped((TOKENS, 2 * UNITS)),
            lump,
            lump,
            first,
            *moved,
        ],
        [],
        *acts,
        *wides,
        *downs,
    )
    cot_pieces, both, hidden, low, high, out_moved = tie(
        (cot_pieces, both, hidden, low, high, out_moved)
    )

    out_moved = back(out_moved)
    far_low = swap(low)
    near, away, grad_first, *grad_moved = call(
        backward_kernel,
        [shaped((TOKENS, TRIPLE)), shaped((TOKENS, WIDTH + TRIPLE)), first, *moved],
        [pltpu.VMEM((2, TOKENS, 2 * UNITS), BF16)],
        *cot_pieces,
        *wides,
        *downs,
        both,
        hidden,
    )
    out_tiles = call(
        collect_kernel,
        [shaped((FAR, SIDE, LANES))],
        [strip],
        out_first,
        *out_moved,
        limit=SMALL_BYTES,
    )[0]
    out_tiles, far_low, near, away, high = tie((out_tiles, far_low, near, away, high))

    grad_moved = back(grad_moved)
    far_high = swap(high)
    away = over(away)
    here = jnp.concatenate([near, away[:, WIDTH:]], axis=0)
    far = swap(here)
    kept = sent = shaped((KEPT, SIDE * SIDE))
    keep_down, send_down = call(
        down_grad_kernel,
        [kept, sent],
        [pltpu.VMEM((2, SIDE * SIDE, LANES), F32)],
        *cot_pieces,
        near,
        away,
        select[2],
    )
    send_down, grad_moved, here, far, far_high = tie(
        (send_down, grad_moved, here, far, far_high)
    )

    come_down = swap(send_down)
    acts = [low, high, over(low), over(high), far_low, far_high, over(far_low), over(far_high)]
    tiles = exchange(
        call(
            join_kernel,
            [shaped((FAR, 2, SIDE, LANES))],
            [strip],
            out_tiles,
            grad_first,
            *grad_moved,
            limit=SMALL_BYTES,
        )[0]
    )
    grad = shaped((HALF, 2, SIDE * SIDE), F32)
    gate_grad, up_grad = call(
        wide_grad_kernel,
        [grad, grad],
        [pltpu.VMEM((2, HALF, 2, SIDE * SIDE), F32), pltpu.SemaphoreType.DMA((2,))],
        *acts,
        here,
        far,
        select[:2, :KEPT],
        space=pltpu.HBM,
    )
    layer_out, input_grad = call(
        finish_kernel,
        [shaped((1, WIDTH))] * 2,
        [pltpu.VMEM((SIDE, LANES), F32)],
        tiles,
        limit=SMALL_BYTES,
    )
    layer_out, input_grad, come_down = tie((layer_out, input_grad, come_down))
    down_grad = call(
        settle_kernel,
        [grad],
        [pltpu.VMEM((HALF, 2, SIDE * SIDE), F32), pltpu.SemaphoreType.DMA],
        keep_down,
        come_down,
        space=pltpu.HBM,
    )[0]
    gate_grad, up_grad, down_grad = (
        jnp.swapaxes(grad, 0, 1) for grad in (gate_grad, up_grad, down_grad)
    )
    return (layer_out, input_grad, gate_grad, up_grad, down_grad)


def solution(mesh):
    fine = Mesh(mesh.devices.reshape(2, 8, 4, 2, 2), ("xh", "z", "y", "c", "rep"))
    blk = ("xh", "z", "y", "c")
    placed = (
        P((*blk, "rep"), None),
        P((*blk, "rep"), None),
        P(blk, None, None),
        P(blk, None, None),
        P(blk, None, None),
        P(None, blk, None),
        P(None, blk),
    )
    return jax.shard_map(
        per_device,
        mesh=fine,
        in_specs=placed,
        out_specs=(
            P((*blk, "rep"), None),
            P((*blk, "rep"), None),
            P(blk, "rep", None),
            P(blk, "rep", None),
            P(blk, "rep", None),
        ),
        check_vma=False,
    )
```

```python
import functools

import jax
import jax.numpy as jnp
from jax import lax
from jax.experimental import pallas as pl
from jax.experimental.pallas import tpu as pltpu
from jax.sharding import Mesh
from jax.sharding import PartitionSpec as P

SIDE = 64
LANES = 128
WIDTH = SIDE * LANES
UNITS = 2 * SIDE
TRIPLE = 3 * UNITS
HALF = 36
KEPT = 2 * HALF
ROWS = 16
TOKENS = 4 * ROWS
FAR = 16
SHIFTS = (1, 3, 2)
VMEM_BYTES = 14 * 1024 * 1024
SMALL_BYTES = 8 * 1024 * 1024
BF16 = jnp.bfloat16
F32 = jnp.float32
NT = (((1,), (1,)), ((), ()))


def call(kernel, outs, scratch, *operands, inside=(), space=pltpu.VMEM, limit=VMEM_BYTES):
    inside = dict(inside)
    return pl.pallas_call(
        kernel,
        out_shape=outs,
        in_specs=[
            pl.BlockSpec(memory_space=inside.get(place, pltpu.VMEM))
            for place in range(len(operands))
        ],
        out_specs=[pl.BlockSpec(memory_space=space)] * len(outs),
        scratch_shapes=scratch,
        compiler_params=pltpu.CompilerParams(vmem_limit_bytes=limit),
        cost_estimate=pl.CostEstimate(flops=0, bytes_accessed=100_000, transcendentals=0),
    )(*operands)


def span(step, width):
    return pl.ds(pl.multiple_of(step * width, width), width)


def spread_kernel(act_ref, cot_ref, out_ref, strip_ref):
    for which, row_ref in enumerate((act_ref, cot_ref)):
        row = row_ref[...].astype(F32)
        for part in range(SIDE):
            strip_ref[part : part + 1, :] = row[:, part * LANES : (part + 1) * LANES]
        turned_row = strip_ref[...].T
        tile = jnp.concatenate([turned_row[:SIDE], turned_row[SIDE:]], axis=1).astype(BF16)
        for place in range(FAR):
            out_ref[place, which] = tile


def gather_kernel(tiles_ref, act_ref, cot_ref, strip_ref):
    for which, out_ref in enumerate((act_ref, cot_ref)):
        for place in range(FAR):
            strip_ref[which, place * SIDE : (place + 1) * SIDE, :] = tiles_ref[
                place, which
            ].astype(F32)
        for inner in range(SIDE):
            out_ref[:, inner * LANES : (inner + 1) * LANES] = strip_ref[
                which, pl.ds(inner, FAR, SIDE), :
            ].astype(BF16)


def summed(first_ref, moved, strip_ref, tiles_ref):
    for inner in range(SIDE):
        cols = slice(inner * LANES, (inner + 1) * LANES)
        total = first_ref[:, cols]
        for ref in moved:
            total = total + ref[:, cols].astype(F32)
        strip_ref[pl.ds(inner, FAR, SIDE), :] = total
    for place in range(FAR):
        tiles_ref[place] = strip_ref[place * SIDE : (place + 1) * SIDE, :].astype(BF16)


def collect_kernel(first_ref, *refs):
    *moved, tiles_ref, strip_ref = refs
    summed(first_ref, moved, strip_ref, tiles_ref)


def join_kernel(out_ref, first_ref, *refs):
    *moved, tiles_ref, strip_ref = refs
    tiles_ref[:, 0] = out_ref[...]
    summed(first_ref, moved, strip_ref, tiles_ref.at[:, 1])


def finish_kernel(total_ref, out_ref, grad_ref, strip_ref):
    for which, row_ref in enumerate((out_ref, grad_ref)):
        total = total_ref[0, which].astype(F32)
        for place in range(1, FAR):
            total = total + total_ref[place, which].astype(F32)
        strip_ref[...] = jnp.concatenate([total[:, :SIDE], total[:, SIDE:]], axis=0).T
        for part in range(SIDE):
            row_ref[:, part * LANES : (part + 1) * LANES] = strip_ref[
                part : part + 1, :
            ].astype(BF16)


def lane_of(block):
    return (block & 1) * SIDE + (block >> 1)


def one_hot(index_ref, count_ref, matrix, unit):
    entries = index_ref[matrix, unit : unit + 1, :]
    shape = (LANES, entries.shape[1])
    rows = lax.broadcasted_iota(jnp.int32, shape, 0)
    live = lax.broadcasted_iota(jnp.int32, shape, 1) < count_ref[matrix, unit]
    return jnp.where((rows == lane_of(entries)) & live, 1.0, 0.0).astype(BF16)


def densify_wide_kernel(index_ref, count_ref, gate_ref, up_ref, wide_ref):
    picks = [[one_hot(index_ref, count_ref, matrix, unit) for unit in range(2)] for matrix in range(2)]

    def spread(step, carry):
        cols = span(step, 4 * SIDE)
        for matrix, blocks_ref in enumerate((gate_ref, up_ref)):
            first, second = (
                jnp.dot(
                    picks[matrix][unit],
                    blocks_ref[unit, :, cols],
                    preferred_element_type=F32,
                ).astype(BF16)
                for unit in range(2)
            )
            for inner in range(4):
                part = slice(inner * SIDE, (inner + 1) * SIDE)
                wide_ref[
                    span(step * 4 + inner, LANES), matrix * UNITS : (matrix + 1) * UNITS
                ] = jnp.concatenate([first[:, part], second[:, part]], axis=1)
        return carry

    lax.fori_loop(0, 16, spread, 0, unroll=2)


def densify_down_kernel(index_ref, count_ref, down_ref, dense_ref, strip_ref):
    for unit in range(2):
        pick = one_hot(index_ref, count_ref, 2, unit)

        def turn(step, carry, unit=unit, pick=pick):
            dense = jnp.dot(
                pick,
                down_ref[unit, :, span(step, 256)],
                preferred_element_type=F32,
            )
            strip_ref[unit, span(step, 256), :] = dense.T
            return carry

        lax.fori_loop(0, 16, turn, 0, unroll=2)

    def gather(inner, carry):
        dense_ref[:, span(inner, LANES)] = jnp.concatenate(
            [strip_ref[unit, pl.ds(inner, SIDE, SIDE), :] for unit in range(2)], axis=0
        ).astype(BF16)
        return carry

    lax.fori_loop(0, SIDE, gather, 0, unroll=8)


def joined(pieces, cols):
    return jnp.concatenate([piece[:, cols] for piece in pieces], axis=0)


def put(first_ref, moved, cols, values):
    first_ref[:, cols] = values[:ROWS]
    for slot, ref in enumerate(moved):
        ref[:, cols] = values[(slot + 1) * ROWS : (slot + 2) * ROWS].astype(BF16)


def forward_kernel(*refs):
    pieces = refs[:4]
    wides, downs = refs[4:6], refs[6:8]
    both_ref, hidden_ref, low_ref, high_ref, first_ref, *moved = refs[8:]

    def project(step, totals):
        cols = span(step, 1024)
        rows = joined(pieces, cols)
        return tuple(
            total + jnp.dot(rows, wide_ref[cols, :], preferred_element_type=F32)
            for total, wide_ref in zip(totals, wides)
        )

    zeros = jnp.zeros((TOKENS, 2 * UNITS), F32)
    totals = lax.fori_loop(0, 8, project, (zeros, zeros), unroll=2)
    hidden = []
    for core, both in enumerate(totals):
        both_ref[core] = both
        gate, upper = both[:, :UNITS], both[:, UNITS:]
        hidden.append((gate * jax.nn.sigmoid(gate) * upper).astype(BF16))
    hidden = jnp.concatenate(hidden, axis=1)
    hidden_ref[...] = hidden

    def outward(step, carry):
        cols = span(step, 512)
        weights = jnp.concatenate([down_ref[:, cols] for down_ref in downs], axis=0)
        put(first_ref, moved, cols, jnp.dot(hidden, weights, preferred_element_type=F32))
        low_ref[:, cols] = joined(pieces[:2], cols)
        high_ref[:, cols] = joined(pieces[2:], cols)
        return carry

    lax.fori_loop(0, 16, outward, 0, unroll=2)


def backward_kernel(*refs):
    pieces = refs[:4]
    wides, downs = refs[4:6], refs[6:8]
    both_ref, hidden_ref, near_ref, away_ref, first_ref, *moved, back_ref = refs[8:]

    def project(step, total):
        cols = span(step, 1024)
        weights = jnp.concatenate([down_ref[:, cols] for down_ref in downs], axis=0)
        return total + lax.dot_general(
            joined(pieces, cols), weights, NT, preferred_element_type=F32
        )

    hidden_grads = lax.fori_loop(0, 8, project, jnp.zeros((TOKENS, 2 * UNITS), F32), unroll=2)
    for core, (small_ref, start) in enumerate(((near_ref, 0), (away_ref, WIDTH))):
        hidden_grad = hidden_grads[:, core * UNITS : (core + 1) * UNITS]
        gate, upper = both_ref[core, :, :UNITS], both_ref[core, :, UNITS:]
        sigmoid_gate = jax.nn.sigmoid(gate)
        gate_cot = hidden_grad * upper * sigmoid_gate * (1.0 + gate * (1.0 - sigmoid_gate))
        up_cot = hidden_grad * (gate * sigmoid_gate)
        cots = jnp.concatenate([gate_cot, up_cot], axis=1).astype(BF16)
        back_ref[core] = cots
        small_ref[:, start : start + UNITS] = hidden_ref[:, core * UNITS : (core + 1) * UNITS]
        small_ref[:, start + UNITS : start + TRIPLE] = cots

    def outward(step, carry):
        cols = span(step, 512)
        values = sum(
            lax.dot_general(back_ref[core], wide_ref[cols, :], NT, preferred_element_type=F32)
            for core, wide_ref in enumerate(wides)
        )
        put(first_ref, moved, cols, values)
        away_ref[:, cols] = joined(pieces, cols)
        return carry

    lax.fori_loop(0, 16, outward, 0, unroll=2)


def turned(values):
    return jnp.concatenate(values, axis=0).astype(F32).T.astype(BF16)


def down_grad_kernel(*refs):
    pieces = (*refs[:4], refs[5])
    near_ref, away_ref, select_ref, keep_ref, send_ref, strip_ref = refs[4:]
    hidden = turned([near_ref[:, :UNITS], away_ref[:, WIDTH : WIDTH + UNITS]])

    def dense(step, carry):
        values = jnp.dot(
            hidden, joined(pieces, span(step, 512)), preferred_element_type=F32
        )
        for part in range(4):
            for unit in range(2):
                strip_ref[unit, pl.ds(step * 4 + part, SIDE, SIDE), :] = values[
                    unit * SIDE : (unit + 1) * SIDE, part * LANES : (part + 1) * LANES
                ]
        return carry

    lax.fori_loop(0, 16, dense, 0, unroll=2)

    def pick(step, carry):
        cols = span(step, 256)
        rows = jnp.concatenate([strip_ref[0, cols, :], strip_ref[1, cols, :]], axis=1)
        values = lax.dot_general(
            select_ref[...], rows.astype(BF16), NT, preferred_element_type=F32
        ).astype(BF16)
        keep_ref[:, cols] = values[:KEPT]
        send_ref[:, cols] = values[KEPT:]
        return carry

    lax.fori_loop(0, 16, pick, 0, unroll=2)


def paired(total_ref, cols, values):
    for entry in range(HALF):
        total_ref[entry, :, cols] = values[2 * entry : 2 * entry + 2]


def wide_grad_kernel(*refs):
    pieces = refs[:8]
    here_ref, far_ref, select_ref, gate_ref, up_ref, total_ref, done = refs[8:]
    cots = turned([here_ref[:, UNITS:], far_ref[:, UNITS:]])

    def step_of(step, carry):
        values = jnp.dot(
            cots, joined(pieces, span(step, 512)), preferred_element_type=F32
        ).astype(BF16)
        for matrix in range(2):
            rows = jnp.concatenate(
                [
                    jnp.concatenate(
                        [
                            values[
                                matrix * UNITS + unit * SIDE : matrix * UNITS + (unit + 1) * SIDE,
                                part * LANES : (part + 1) * LANES,
                            ]
                            for unit in range(2)
                        ],
                        axis=1,
                    )
                    for part in range(4)
                ],
                axis=0,
            )
            picked = lax.dot_general(select_ref[matrix], rows, NT, preferred_element_type=F32)
            paired(total_ref.at[matrix], span(step, 256), picked)
        return carry

    lax.fori_loop(0, 16, step_of, 0, unroll=2)
    copies = [
        pltpu.make_async_copy(total_ref.at[place], out_ref, done.at[place])
        for place, out_ref in enumerate((gate_ref, up_ref))
    ]
    for copy in copies:
        copy.start()
    for copy in copies:
        copy.wait()


def settle_kernel(keep_ref, send_ref, out_ref, total_ref, done):
    def settle(step, carry):
        cols = span(step, 512)
        paired(total_ref, cols, keep_ref[:, cols].astype(F32) + send_ref[:, cols].astype(F32))
        return carry

    lax.fori_loop(0, 8, settle, 0)
    copy = pltpu.make_async_copy(total_ref, out_ref, done)
    copy.start()
    copy.wait()


def ring(size, shift):
    return [(place, (place + shift) % size) for place in range(size)]


def per_device(
    activations, out_cotangent, gate_blocks, up_blocks, down_blocks, block_index, block_counts
):
    length = gate_blocks.shape[1]
    def shaped(dims, kind=BF16):
        return jax.ShapeDtypeStruct(dims, kind)

    def along(first):
        return [first] + [lax.ppermute(first, "y", ring(4, shift)) for shift in SHIFTS]

    def over(piece):
        return lax.ppermute(piece, "c", ring(2, 1))

    def swap(piece):
        return lax.ppermute(piece, "rep", ring(2, 1))

    def back(moved):
        return [
            lax.ppermute(part, "y", ring(4, -shift)) for part, shift in zip(moved, SHIFTS)
        ]

    tie = lax.optimization_barrier
    numbers = (block_index, block_counts)
    strips = pltpu.VMEM((2, SIDE * FAR, LANES), F32)
    strip = pltpu.VMEM((SIDE * FAR, LANES), F32)

    def exchange(tiles):
        return lax.all_to_all(tiles, ("xh", "z"), 0, 0, tiled=True)

    tiles = call(
        spread_kernel,
        [shaped((FAR, 2, SIDE, LANES))],
        [pltpu.VMEM((SIDE, LANES), F32)],
        activations,
        out_cotangent,
        limit=62 * 1024 * 1024,
    )[0]
    tiles = exchange(tiles)
    down = call(
        densify_down_kernel,
        [shaped((UNITS, WIDTH))],
        [pltpu.VMEM((2, SIDE * SIDE, LANES), F32)],
        *numbers,
        down_blocks,
        inside={1: pltpu.SMEM},
    )[0]
    wide = call(
        densify_wide_kernel,
        [shaped((WIDTH, 2 * UNITS))],
        [],
        *numbers,
        gate_blocks,
        up_blocks,
        inside={1: pltpu.SMEM},
    )[0]
    tiles, wide, down, block_index = tie((tiles, wide, down, block_index))
    act_first, cot_first = call(
        gather_kernel, [shaped((ROWS, WIDTH))] * 2, [strips], tiles, limit=SMALL_BYTES
    )
    acts = along(act_first)
    wides, downs = (wide, over(wide)), (down, over(down))
    live = jnp.arange(length)[None, None, :] < block_counts[:, :, None]
    places = jnp.where(live, lane_of(block_index), -1)
    halves = places.reshape(3, 2, 2, HALF)
    halves = jnp.where(lax.axis_index("rep") == 0, halves, halves[:, :, ::-1])
    halves = jnp.transpose(halves, (0, 2, 3, 1))
    goal = jnp.where(halves >= 0, halves + LANES * jnp.arange(2), -1)
    select = (goal.reshape(3, 2 * KEPT)[:, :, None] == jnp.arange(2 * LANES)).astype(BF16)

    cot_pieces = along(cot_first)
    first, moved = shaped((ROWS, WIDTH), F32), [shaped((ROWS, WIDTH))] * 3
    lump = shaped((2 * ROWS, WIDTH))
    both, hidden, low, high, out_first, *out_moved = call(
        forward_kernel,
        [
            shaped((2, TOKENS, 2 * UNITS), F32),
            shaped((TOKENS, 2 * UNITS)),
            lump,
            lump,
            first,
            *moved,
        ],
        [],
        *acts,
        *wides,
        *downs,
    )
    cot_pieces, both, hidden, low, high, out_moved = tie(
        (cot_pieces, both, hidden, low, high, out_moved)
    )

    out_moved = back(out_moved)
    far_low = swap(low)
    near, away, grad_first, *grad_moved = call(
        backward_kernel,
        [shaped((TOKENS, TRIPLE)), shaped((TOKENS, WIDTH + TRIPLE)), first, *moved],
        [pltpu.VMEM((2, TOKENS, 2 * UNITS), BF16)],
        *cot_pieces,
        *wides,
        *downs,
        both,
        hidden,
    )
    out_tiles = call(
        collect_kernel,
        [shaped((FAR, SIDE, LANES))],
        [strip],
        out_first,
        *out_moved,
        limit=SMALL_BYTES,
    )[0]
    out_tiles, far_low, near, away, high = tie((out_tiles, far_low, near, away, high))

    grad_moved = back(grad_moved)
    far_high = swap(high)
    away = over(away)
    here = jnp.concatenate([near, away[:, WIDTH:]], axis=0)
    far = swap(here)
    kept = sent = shaped((KEPT, SIDE * SIDE))
    keep_down, send_down = call(
        down_grad_kernel,
        [kept, sent],
        [pltpu.VMEM((2, SIDE * SIDE, LANES), F32)],
        *cot_pieces,
        near,
        away,
        select[2],
    )
    send_down, grad_moved, here, far, far_high = tie(
        (send_down, grad_moved, here, far, far_high)
    )

    come_down = swap(send_down)
    acts = [low, high, over(low), over(high), far_low, far_high, over(far_low), over(far_high)]
    tiles = exchange(
        call(
            join_kernel,
            [shaped((FAR, 2, SIDE, LANES))],
            [strip],
            out_tiles,
            grad_first,
            *grad_moved,
            limit=SMALL_BYTES,
        )[0]
    )
    grad = shaped((HALF, 2, SIDE * SIDE), F32)
    gate_grad, up_grad = call(
        wide_grad_kernel,
        [grad, grad],
        [pltpu.VMEM((2, HALF, 2, SIDE * SIDE), F32), pltpu.SemaphoreType.DMA((2,))],
        *acts,
        here,
        far,
        select[:2, :KEPT],
        space=pltpu.HBM,
    )
    layer_out, input_grad = call(
        finish_kernel,
        [shaped((1, WIDTH))] * 2,
        [pltpu.VMEM((SIDE, LANES), F32)],
        tiles,
        limit=SMALL_BYTES,
    )
    layer_out, input_grad, come_down = tie((layer_out, input_grad, come_down))
    down_grad = call(
        settle_kernel,
        [grad],
        [pltpu.VMEM((HALF, 2, SIDE * SIDE), F32), pltpu.SemaphoreType.DMA],
        keep_down,
        come_down,
        space=pltpu.HBM,
    )[0]
    gate_grad, up_grad, down_grad = (
        jnp.swapaxes(grad, 0, 1) for grad in (gate_grad, up_grad, down_grad)
    )
    return (layer_out, input_grad, gate_grad, up_grad, down_grad)


def solution(mesh):
    fine = Mesh(mesh.devices.reshape(2, 8, 4, 2, 2), ("xh", "z", "y", "c", "rep"))
    blk = ("xh", "z", "y", "c")
    placed = (
        P((*blk, "rep"), None),
        P((*blk, "rep"), None),
        P(blk, None, None),
        P(blk, None, None),
        P(blk, None, None),
        P(None, blk, None),
        P(None, blk),
    )
    return jax.shard_map(
        per_device,
        mesh=fine,
        in_specs=placed,
        out_specs=(
            P((*blk, "rep"), None),
            P((*blk, "rep"), None),
            P(blk, "rep", None),
            P(blk, "rep", None),
            P(blk, "rep", None),
        ),
        check_vma=False,
    )
```
